32 devices in a mesh: grp: 2 (over x), loop: 16 (over z, y, core).
Axes of the slice: x: 2, y: 2, z: 4, core: 2. Of those that a mesh axis runs over, the one named last changes fastest.
Arguments:
- hidden: bfloat16 [2, 256, 14848], P(None, ('grp', 'loop')), parts along dimension 1, may hold values from -6 to 6
- lengths: int32 [256], P(('grp', 'loop')), parts along dimension 0, may hold values from 1 to 256, as said below
- cache_keys: bfloat16 [256, 256, 64], P(('grp', 'loop')), parts along dimension 0, may hold values from -600 to 600
- cache_values: bfloat16 [256, 256, 64], P(('grp', 'loop')), parts along dimension 0, may hold values from -6 to 6
- ln_gain: float32 [14848], replicated, may hold values from 0.5 to 1.5
- ln_bias: float32 [14848], replicated, may hold values from -3 to 3
- w_qkv: bfloat16 [14848, 1984], P('loop'), may hold values from -0.046875 to 0.046875
- w_out: bfloat16 [1856, 14848], P(None, 'loop'), may hold values from -0.125 to 0.125
Outputs:
- results: bfloat16 [2, 256, 14848], P(None, ('grp', 'loop')), parts along dimension 1
The draws below stay inside these ranges and needn't reach their ends.
There are 2 independent parts, one for each index of `grp`. The reference program is written for one: setup_inputs(seed, part) draws one part's arguments, and reference() takes and returns one part's arrays. A program takes and returns all parts, laid end to end along the dimension named above; an argument that names none is the same for every part. Nothing has to cross between parts.
Inputs may be any that keep to these rules, and one draw needn't show every extreme that they name: `lengths`: every row has at least one filled position; some row of every draw has all 256 filled and some row has one.
All inputs are finite; a program needn't handle non-finite values.
Results may differ from the reference program's by a relative error of at most 0.012.
Values may be sent and summed in bfloat16 or wider, within the bound.
A program may use at most 64 MiB of HBM per device.

```python
import jax
import jax.numpy as jnp
from jax import lax

D = 14848
HEAD = 64
HEADS = 29
CTX = 256
STEPS = 2
ROWS = 128


def draw_lengths(key, part):
    key = jax.random.fold_in(key, 7)
    first_key, second_key = jax.random.split(key)
    drawn = jax.random.randint(first_key, (ROWS,), 1, CTX + 1)
    picks = jax.random.permutation(second_key, ROWS)
    drawn = drawn.at[picks[0]].set(CTX).at[picks[1]].set(1)
    return drawn.astype(jnp.int32)


def draw_cache_keys(key, part):
    key = jax.random.fold_in(key, 11)
    first_key = jax.random.fold_in(key, 0)
    base = jnp.clip(jax.random.normal(first_key, (ROWS, CTX, HEAD), jnp.float32), -6.0, 6.0)
    return base.astype(jnp.bfloat16)


def levels(stream_key, extent, cuts, low, top_value):
    def one(dim, parts):
        steps = jax.random.uniform(jax.random.fold_in(jax.random.fold_in(stream_key, 6), dim), (parts,), jnp.float32, low / len(cuts), top_value / len(cuts))
        return jnp.repeat(jnp.exp(steps), extent[dim] // parts).reshape((-1,) + (1,) * (len(extent) - dim - 1))

    gain = one(*cuts[0])
    for cut in cuts[1:]:
        gain = gain * one(*cut)
    return gain


def normal_values(own_key, extent, scale, bound, shards=(), kind=jnp.bfloat16):
    gain = levels(own_key, extent, shards, -0.22, 0.18) if shards else 1.0
    values = jax.random.normal(own_key, extent, jnp.float32) * scale * gain
    return jnp.minimum(jnp.maximum(values, -bound), bound).astype(kind)


def setup_inputs(seed: int = 0, part: int = 0) -> dict:
    streams_of = jax.random.split(jax.random.key(seed), 9)
    part_splits = jax.random.split(jax.random.fold_in(streams_of[8], part), 9)
    hidden = normal_values(part_splits[0], (STEPS, ROWS, D), 1.0, 6.0, ((1, 16),))
    lengths = draw_lengths(jax.random.fold_in(jax.random.fold_in(streams_of[8], part), 71), part)
    cache_keys = draw_cache_keys(jax.random.fold_in(jax.random.fold_in(streams_of[8], part), 71), part)
    cache_values = normal_values(part_splits[3], (ROWS, CTX, HEAD), 1.0, 6.0, ((0, 16),))
    ln_gain = jnp.clip(1.0 + 0.1 * jax.random.normal(streams_of[4], (D,), jnp.float32), 0.5, 1.5)
    ln_bias = normal_values(streams_of[5], (D,), 0.5, 3.0, (), jnp.float32)
    w_qkv = normal_values(streams_of[6], (D, (HEADS + 2) * HEAD), D ** -0.5, 0.046875, ((0, 16),))
    w_out = normal_values(streams_of[7], (HEADS * HEAD, D), (HEADS * HEAD) ** -0.5, 0.125, ((1, 16),))
    return {"hidden": hidden, "lengths": lengths, "cache_keys": cache_keys, "cache_values": cache_values, "ln_gain": ln_gain, "ln_bias": ln_bias, "w_qkv": w_qkv, "w_out": w_out}


def layer_norm(current, ln_gain, ln_bias):
    values = current.astype(jnp.float32)
    average = lax.optimization_barrier(jnp.mean(values, axis=-1, keepdims=True))
    centred = values - average
    variance = lax.optimization_barrier(jnp.mean(centred * centred, axis=-1, keepdims=True))
    return (centred * lax.rsqrt(variance + 1e-05) * ln_gain + ln_bias).astype(jnp.bfloat16)

def attend(queries, all_keys, all_values, visible):
    scores = jnp.einsum('rhe,rpe->rhp', queries.astype(jnp.float32), all_keys.astype(jnp.float32)) * 0.125
    scores = jnp.where(visible[:, None, :], scores, -1e+30)
    maxima = lax.optimization_barrier(jnp.max(scores, axis=-1, keepdims=True))
    exps = jnp.where(visible[:, None, :], jnp.exp(scores - maxima), 0.0)
    totals = lax.optimization_barrier(jnp.sum(exps, axis=-1, keepdims=True))
    probs = (exps / totals).astype(jnp.bfloat16)
    mixed = jnp.einsum('rhp,rpe->rhe', probs.astype(jnp.float32), all_values.astype(jnp.float32))
    return mixed.reshape(mixed.shape[0], -1).astype(jnp.bfloat16)

def reference(hidden, lengths, cache_keys, cache_values, ln_gain, ln_bias, w_qkv, w_out):
    visible_cache = jnp.arange(CTX, dtype=jnp.int32)[None, :] < lengths[:, None]
    fresh_keys = []
    fresh_values = []
    results = []
    for step_index in range(STEPS):
        current = hidden[step_index]
        normed = layer_norm(current, ln_gain, ln_bias)
        projected = jnp.dot(normed, w_qkv, preferred_element_type=jnp.float32).astype(jnp.bfloat16)
        queries = projected[:, :HEADS * HEAD].reshape(ROWS, HEADS, HEAD)
        fresh_keys.append(projected[:, HEADS * HEAD:(HEADS + 1) * HEAD])
        fresh_values.append(projected[:, (HEADS + 1) * HEAD:])
        all_keys = jnp.concatenate([cache_keys, jnp.stack(fresh_keys, 1)], 1)
        all_values = jnp.concatenate([cache_values, jnp.stack(fresh_values, 1)], 1)
        visible = jnp.concatenate([visible_cache, jnp.ones((ROWS, step_index + 1), bool)], 1)
        mixed_heads = attend(queries, all_keys, all_values, visible)
        attention = jnp.dot(mixed_heads, w_out, preferred_element_type=jnp.float32).astype(jnp.bfloat16)
        results.append((current.astype(jnp.float32) + attention.astype(jnp.float32)).astype(jnp.bfloat16))
    return jnp.stack(results)
```

```python
import jax
import jax.numpy as jnp
from jax import lax
from jax.sharding import PartitionSpec as P


def layer_norm(current, ln_gain, ln_bias):
    values = current.astype(jnp.float32)
    average = jnp.mean(values, axis=-1, keepdims=True)
    centred = values - average
    variance = jnp.mean(centred * centred, axis=-1, keepdims=True)
    return (centred * lax.rsqrt(variance + 1e-05) * ln_gain + ln_bias).astype(jnp.bfloat16)


def attend(queries, fresh_keys, fresh_values, cache_keys, cache_values, lengths):
    rows, steps, heads, head_dim = queries.shape
    context = cache_keys.shape[1]
    flat = queries.reshape(rows, steps * heads, head_dim)
    seen = jnp.arange(context, dtype=jnp.int32)[None, :] < lengths[:, None]
    old = jnp.einsum("rqe,rpe->rqp", flat, cache_keys, preferred_element_type=jnp.float32) * 0.125
    old = jnp.where(seen[:, None, :], old, -1e30)
    new = jnp.einsum("rqe,rte->rqt", flat, fresh_keys, preferred_element_type=jnp.float32) * 0.125
    step_of = jnp.arange(steps * heads, dtype=jnp.int32)[:, None] // heads
    seen_new = jnp.arange(steps, dtype=jnp.int32)[None, :] <= step_of
    new = jnp.where(seen_new[None], new, -1e30)
    maxima = jnp.maximum(
        jnp.max(old, axis=-1, keepdims=True), jnp.max(new, axis=-1, keepdims=True)
    )
    exp_old = jnp.exp(old - maxima)
    exp_new = jnp.exp(new - maxima)
    totals = jnp.sum(exp_old, axis=-1, keepdims=True) + jnp.sum(exp_new, axis=-1, keepdims=True)
    prob_old = (exp_old / totals).astype(jnp.bfloat16)
    prob_new = (exp_new / totals).astype(jnp.bfloat16)
    mixed = jnp.einsum("rqp,rpe->rqe", prob_old, cache_values, preferred_element_type=jnp.float32)
    mixed += jnp.einsum("rqt,rte->rqe", prob_new, fresh_values, preferred_element_type=jnp.float32)
    return mixed.reshape(rows, steps, heads * head_dim).astype(jnp.bfloat16)


def local(hidden, lengths, cache_keys, cache_values, ln_gain, ln_bias, w_qkv, w_out):
    steps, rows, width = hidden.shape
    head_dim = cache_keys.shape[2]
    heads = w_qkv.shape[1] // head_dim - 2
    count = lax.axis_size("loop")
    part = width // count
    normed = layer_norm(hidden, ln_gain, ln_bias).reshape(steps * rows, width)
    spread = lax.all_to_all(normed, "loop", split_axis=1, concat_axis=0, tiled=True)
    terms = jnp.dot(spread, w_qkv, preferred_element_type=jnp.float32).astype(jnp.bfloat16)
    terms = terms.reshape(count, steps * rows, -1)
    arrived = lax.all_to_all(terms, "loop", split_axis=0, concat_axis=0, tiled=True)
    projected = jnp.sum(arrived.astype(jnp.float32), axis=0).astype(jnp.bfloat16)
    projected = projected.reshape(steps, rows, -1).transpose(1, 0, 2)
    queries = projected[:, :, : heads * head_dim].reshape(rows, steps, heads, head_dim)
    fresh_keys = projected[:, :, heads * head_dim : (heads + 1) * head_dim]
    fresh_values = projected[:, :, (heads + 1) * head_dim :]
    mixed = attend(queries, fresh_keys, fresh_values, cache_keys, cache_values, lengths)
    mixed = mixed.transpose(1, 0, 2).reshape(steps * rows, -1)
    every_row = lax.all_gather(mixed, "loop", axis=0, tiled=True)
    columns = jnp.dot(every_row, w_out, preferred_element_type=jnp.float32).astype(jnp.bfloat16)
    attention = lax.all_to_all(columns, "loop", split_axis=0, concat_axis=1, tiled=True)
    attention = attention.reshape(steps, rows, width)
    return (hidden.astype(jnp.float32) + attention.astype(jnp.float32)).astype(jnp.bfloat16)


def solution(mesh):
    return jax.shard_map(
        local,
        mesh=mesh,
        in_specs=(
            P(None, ("grp", "loop"), None),
            P(("grp", "loop")),
            P(("grp", "loop"), None, None),
            P(("grp", "loop"), None, None),
            P(),
            P(),
            P("loop", None),
            P(None, "loop"),
        ),
        out_specs=P(None, ("grp", "loop"), None),
        check_vma=False,
    )
```

```python
import functools

import jax
import jax.numpy as jnp
from jax import lax
from jax.experimental import pallas as pl
from jax.experimental.pallas import tpu as pltpu
from jax.sharding import PartitionSpec as P

MESH = pl.DeviceIdType.MESH
VMEM = pltpu.VMEM
DMA = pltpu.SemaphoreType.DMA


def hail(devices):
    barrier = pltpu.get_barrier_semaphore()
    for device in devices:
        pl.semaphore_signal(barrier, inc=1, device_id={"loop": device}, device_id_type=MESH)


def meet(devices):
    pl.semaphore_wait(pltpu.get_barrier_semaphore(), len(devices))


def remote(src, dst, send_sem, recv_sem, device):
    return pltpu.make_async_remote_copy(
        src_ref=src,
        dst_ref=dst,
        send_sem=send_sem,
        recv_sem=recv_sem,
        device_id={"loop": device},
        device_id_type=MESH,
    )


def far_first(count):
    return sorted(range(1, count), key=lambda k: abs(2 * k - count))


def product(left, weights, store):
    width = weights.shape[1]
    for low in range(0, width, 512):
        high = min(low + 512, width)
        store(
            low,
            high,
            jnp.dot(left, weights[:, low:high], preferred_element_type=jnp.float32),
        )


def project_kernel(
    count,
    h_ref,
    gain_ref,
    bias_ref,
    w_hbm,
    o_ref,
    w_ref,
    normed,
    spread,
    terms,
    sib,
    packed,
    arrived,
    w_sem,
    send_x,
    recv_x,
    send_a,
    recv_a,
    send_b,
    recv_b,
):
    me = lax.axis_index("loop")
    chips = count // 2
    core = lax.rem(me, 2)
    chip = me // 2
    other = 1 - core
    sibling = chip * 2 + other
    part = w_ref.shape[0]
    rows, width = h_ref.shape
    far = far_first(count)
    everyone = [lax.rem(me + k, count) for k in far]
    hail(everyone)
    w_copy = pltpu.make_async_copy(w_hbm, w_ref, w_sem)
    w_copy.start()
    values = h_ref[...].astype(jnp.float32)
    average = jnp.sum(values, axis=-1, keepdims=True) / width
    centred = values - average
    variance = jnp.sum(centred * centred, axis=-1, keepdims=True) / width
    scale = lax.rsqrt(variance + 1e-05)
    for d in range(count):
        at = slice(d * part, (d + 1) * part)
        block = (h_ref[:, at].astype(jnp.float32) - average) * scale
        normed[d] = (block * gain_ref[:, at] + bias_ref[:, at]).astype(jnp.bfloat16)
    meet(everyone)
    copies = []
    for k in far:
        to = lax.rem(me + k, count)
        copy = remote(normed.at[to], spread.at[core, chip], send_x.at[k], recv_x.at[k], to)
        copy.start()
        copies.append(copy)
    spread[core, chip] = normed[me]
    w_copy.wait()
    for k in far:
        sender = lax.rem(me + count - k, count)
        block = spread.at[lax.rem(sender, 2), sender // 2]
        remote(block, block, send_x.at[k], recv_x.at[k], sender).wait_recv()

    def multiply(which):
        def store(low, high, tile):
            terms[which, :, :, low:high] = tile.reshape(chips, rows, high - low)

        product(spread[which].reshape(chips * rows, part), w_ref, store)

    multiply(other)
    order = far_first(chips)
    firsts = {}
    for k in order + [0]:
        j = lax.rem(chip + k, chips)
        firsts[k] = remote(terms.at[other, j], sib.at[j], send_a.at[k], recv_a.at[k], sibling)
        firsts[k].start()
    multiply(core)
    for k in order:
        j = lax.rem(chip + k, chips)
        firsts[k].wait_recv()
        packed[j] = (terms[core, j] + sib[j]).astype(jnp.bfloat16)
        copy = remote(packed.at[j], arrived.at[chip], send_b.at[k], recv_b.at[k], j * 2 + core)
        copy.start()
        copies.append(copy)
    firsts[0].wait_recv()
    total = terms[core, chip] + sib[chip]
    for k in order[::-1]:
        sender = lax.rem(chip + chips - k, chips)
        block = arrived.at[sender]
        remote(block, block, send_b.at[k], recv_b.at[k], sender * 2 + core).wait_recv()
        total = total + arrived[sender].astype(jnp.float32)
    o_ref[...] = total.astype(jnp.bfloat16)
    for copy in list(firsts.values()) + copies:
        copy.wait_send()


def call(kernel, out, specs, scratch, collective_id, *args):
    return pl.pallas_call(
        kernel,
        out_shape=out,
        in_specs=[pl.BlockSpec(memory_space=space) for space in specs],
        out_specs=pl.BlockSpec(memory_space=VMEM),
        scratch_shapes=scratch,
        compiler_params=pltpu.CompilerParams(
            collective_id=collective_id, has_side_effects=True, vmem_limit_bytes=48 * 2**20
        ),
    )(*args)


def project(hidden, ln_gain, ln_bias, w_qkv, count, collective_id):
    rows = hidden.shape[0]
    part, width = w_qkv.shape
    chips = count // 2
    half = jnp.bfloat16
    return call(
        functools.partial(project_kernel, count),
        jax.ShapeDtypeStruct((rows, width), half),
        [VMEM, VMEM, VMEM, pl.ANY],
        [
            VMEM((part, width), half),
            VMEM((count, rows, part), half),
            VMEM((2, chips, rows, part), half),
            VMEM((2, chips, rows, width), jnp.float32),
            VMEM((chips, rows, width), jnp.float32),
            VMEM((chips, rows, width), half),
            VMEM((chips, rows, width), half),
            DMA,
        ]
        + [DMA((count,))] * 2
        + [DMA((chips,))] * 4,
        collective_id,
        hidden,
        ln_gain,
        ln_bias,
        w_qkv,
    )


def output_kernel(
    count,
    m_ref,
    w_hbm,
    o_ref,
    w_ref,
    heads,
    columns,
    w_sem,
    send_a,
    recv_a,
    send_y,
    recv_y,
    send_s,
    recv_s,
    send_x,
    recv_x,
):
    me = lax.axis_index("loop")
    core = lax.rem(me, 2)
    chip = me // 2
    other = 1 - core
    chips = count // 2
    pairs = chips // 2
    pair = chip // 2
    side = lax.rem(chip, 2)
    sibling = chip * 2 + other
    partner = (pair * 2 + 1 - side) * 2 + core
    rows, depth = m_ref.shape
    everyone = [lax.rem(me + k, count) for k in far_first(count)]
    hail(everyone)
    w_copy = pltpu.make_async_copy(w_hbm, w_ref, w_sem)
    w_copy.start()
    meet(everyone)
    order = far_first(pairs)[::-1]
    mine = heads.at[core, chip]
    copies = []

    def push(copy):
        copy.start()
        copies.append(copy)

    push(remote(m_ref, mine, send_y.at[0], recv_y.at[0], partner))
    for k in order[::-1]:
        to = (lax.rem(pair + k, pairs) * 2 + side) * 2 + core
        push(remote(m_ref, mine, send_a.at[k], recv_a.at[k], to))
    push(remote(m_ref, mine, send_s.at[0], recv_s.at[0], sibling))
    heads[core, chip] = m_ref[...]
    source = pair * 2 + 1 - side
    block = heads.at[core, source]
    remote(block, block, send_y.at[0], recv_y.at[0], partner).wait_recv()
    push(remote(block, block, send_s.at[pairs], recv_s.at[pairs], sibling))
    for k in order:
        source = lax.rem(pair + pairs - k, pairs) * 2 + side
        block = heads.at[core, source]
        remote(block, block, send_a.at[k], recv_a.at[k], partner).wait_recv()
        push(remote(block, block, send_y.at[k], recv_y.at[k], partner))
        push(remote(block, block, send_s.at[k], recv_s.at[k], sibling))
    for k in order:
        source = lax.rem(pair + pairs - k, pairs) * 2 + 1 - side
        block = heads.at[core, source]
        remote(block, block, send_y.at[k], recv_y.at[k], partner).wait_recv()
        push(remote(block, block, send_s.at[pairs + k], recv_s.at[pairs + k], sibling))
    w_copy.wait()

    def multiply(which):
        def store(low, high, tile):
            columns[which, :, :, low:high] = tile.astype(jnp.bfloat16).reshape(
                chips, rows, high - low
            )

        product(heads[which].reshape(chips * rows, depth), w_ref, store)

    spans = far_first(chips)
    multiply(core)
    for k in spans:
        j = lax.rem(chip + k, chips)
        sems = send_x.at[k], recv_x.at[k]
        push(remote(columns.at[core, j], o_ref.at[me], *sems, j * 2 + core))
    o_ref[me] = columns[core, chip]
    for far in range(2):
        for k in [0] + order:
            source = lax.rem(pair + pairs - k, pairs) * 2 + (1 - side if far else side)
            block = heads.at[other, source]
            sem = far * pairs + k
            remote(block, block, send_s.at[sem], recv_s.at[sem], sibling).wait_recv()
    multiply(other)
    for k in spans + [0]:
        j = lax.rem(chip + k, chips)
        sems = send_x.at[chips + k], recv_x.at[chips + k]
        push(remote(columns.at[other, j], o_ref.at[me], *sems, j * 2 + other))
    for k in spans:
        sender = lax.rem(chip + chips - k, chips) * 2 + core
        block = o_ref.at[sender]
        remote(block, block, send_x.at[k], recv_x.at[k], sender).wait_recv()
    for k in spans + [0]:
        sender = lax.rem(chip + chips - k, chips) * 2 + other
        block = o_ref.at[sender]
        remote(block, block, send_x.at[chips + k], recv_x.at[chips + k], sender).wait_recv()
    for copy in copies:
        copy.wait_send()


def output(mixed, w_out, count, collective_id):
    rows, depth = mixed.shape
    part = w_out.shape[1]
    chips = count // 2
    half = jnp.bfloat16
    return call(
        functools.partial(output_kernel, count),
        jax.ShapeDtypeStruct((count, rows, part), half),
        [VMEM, pl.ANY],
        [
            VMEM((depth, part), half),
            VMEM((2, chips, rows, depth), half),
            VMEM((2, chips, rows, part), half),
            DMA,
        ]
        + [DMA((chips // 2,))] * 4
        + [DMA((chips,))] * 2
        + [DMA((count,))] * 2,
        collective_id,
        mixed,
        w_out,
    )


def attend(queries, fresh_keys, fresh_values, cache_keys, cache_values, lengths):
    rows, steps, heads, head_dim = queries.shape
    context = cache_keys.shape[1]
    flat = queries.reshape(rows, steps * heads, head_dim)
    seen = jnp.arange(context, dtype=jnp.int32)[None, :] < lengths[:, None]
    old = jnp.einsum("rqe,rpe->rqp", flat, cache_keys, preferred_element_type=jnp.float32) * 0.125
    old = jnp.where(seen[:, None, :], old, -1e30)
    new = jnp.einsum("rqe,rte->rqt", flat, fresh_keys, preferred_element_type=jnp.float32) * 0.125
    step_of = jnp.arange(steps * heads, dtype=jnp.int32)[:, None] // heads
    seen_new = jnp.arange(steps, dtype=jnp.int32)[None, :] <= step_of
    new = jnp.where(seen_new[None], new, -1e30)
    maxima = jnp.maximum(
        jnp.max(old, axis=-1, keepdims=True), jnp.max(new, axis=-1, keepdims=True)
    )
    exp_old = jnp.exp(old - maxima)
    exp_new = jnp.exp(new - maxima)
    totals = jnp.sum(exp_old, axis=-1, keepdims=True) + jnp.sum(exp_new, axis=-1, keepdims=True)
    prob_old = (exp_old / totals).astype(jnp.bfloat16)
    prob_new = (exp_new / totals).astype(jnp.bfloat16)
    mixed = jnp.einsum("rqp,rpe->rqe", prob_old, cache_values, preferred_element_type=jnp.float32)
    mixed += jnp.einsum("rqt,rte->rqe", prob_new, fresh_values, preferred_element_type=jnp.float32)
    return mixed.reshape(rows, steps, heads * head_dim).astype(jnp.bfloat16)


def local(hidden, lengths, cache_keys, cache_values, ln_gain, ln_bias, w_qkv, w_out):
    steps, rows, width = hidden.shape
    head_dim = cache_keys.shape[2]
    heads = w_qkv.shape[1] // head_dim - 2
    count = lax.axis_size("loop")
    both = steps * rows
    projected = project(
        hidden.reshape(both, width), ln_gain[None], ln_bias[None], w_qkv, count, 0
    )
    projected = projected.reshape(steps, rows, -1).transpose(1, 0, 2)
    queries = projected[:, :, : heads * head_dim].reshape(rows, steps, heads, head_dim)
    fresh_keys = projected[:, :, heads * head_dim : (heads + 1) * head_dim]
    fresh_values = projected[:, :, (heads + 1) * head_dim :]
    mixed = attend(queries, fresh_keys, fresh_values, cache_keys, cache_values, lengths)
    mixed = mixed.transpose(1, 0, 2).reshape(steps * rows, -1)
    attention = output(mixed, w_out, count, 1)
    attention = attention.transpose(1, 0, 2).reshape(steps, rows, width)
    return (hidden.astype(jnp.float32) + attention.astype(jnp.float32)).astype(jnp.bfloat16)


def solution(mesh):
    return jax.shard_map(
        local,
        mesh=mesh,
        in_specs=(
            P(None, ("grp", "loop"), None),
            P(("grp", "loop")),
            P(("grp", "loop"), None, None),
            P(("grp", "loop"), None, None),
            P(),
            P(),
            P("loop", None),
            P(None, "loop"),
        ),
        out_specs=P(None, ("grp", "loop"), None),
        check_vma=False,
    )
```

```python
import functools

import jax
import jax.numpy as jnp
from jax import lax
from jax.experimental import pallas as pl
from jax.experimental.pallas import tpu as pltpu
from jax.sharding import PartitionSpec as P

MESH = pl.DeviceIdType.MESH
VMEM = pltpu.VMEM
DMA = pltpu.SemaphoreType.DMA


def hail(devices):
    barrier = pltpu.get_barrier_semaphore()
    for device in devices:
        pl.semaphore_signal(barrier, inc=1, device_id={"loop": device}, device_id_type=MESH)


def meet(devices):
    pl.semaphore_wait(pltpu.get_barrier_semaphore(), len(devices))


def remote(src, dst, send_sem, recv_sem, device):
    return pltpu.make_async_remote_copy(
        src_ref=src,
        dst_ref=dst,
        send_sem=send_sem,
        recv_sem=recv_sem,
        device_id={"loop": device},
        device_id_type=MESH,
    )


def far_first(count):
    return sorted(range(1, count), key=lambda k: abs(2 * k - count))


def product(left, weights, width, columns, store):
    for low in range(0, width, 512):
        high = min(low + 512, width)
        block = weights[:, low:high] if columns else weights[low:high, :]
        dims = (((1,), (1 - columns,)), ((), ()))
        store(
            low, high, lax.dot_general(left, block, dims, preferred_element_type=jnp.float32)
        )


def project_kernel(
    count,
    h_ref,
    gain_ref,
    bias_ref,
    w_hbm,
    o_ref,
    w_ref,
    normed,
    spread,
    terms,
    sib,
    packed,
    arrived,
    w_sem,
    send_x,
    recv_x,
    send_a,
    recv_a,
    send_b,
    recv_b,
):
    me = lax.axis_index("loop")
    chips = count // 2
    core = lax.rem(me, 2)
    chip = me // 2
    other = 1 - core
    sibling = chip * 2 + other
    pairs = chips // 2
    pair = chip // 2
    side = lax.rem(chip, 2)
    partner = (pair * 2 + 1 - side) * 2 + core
    part = w_ref.shape[0]
    rows, width = h_ref.shape
    far = far_first(count)
    everyone = [lax.rem(me + k, count) for k in far]
    hail(everyone)
    w_copy = pltpu.make_async_copy(w_hbm, w_ref, w_sem)
    w_copy.start()
    values = h_ref[...].astype(jnp.float32)
    average = jnp.sum(values, axis=-1, keepdims=True) / width
    centred = values - average
    variance = jnp.sum(centred * centred, axis=-1, keepdims=True) / width
    scale = lax.rsqrt(variance + 1e-05)
    gain = gain_ref[...].reshape(1, width)
    bias = bias_ref[...].reshape(1, width)
    for d in range(count):
        at = slice(d * part, (d + 1) * part)
        block = (h_ref[:, at].astype(jnp.float32) - average) * scale
        normed[d] = (block * gain[:, at] + bias[:, at]).astype(jnp.bfloat16)
    meet(everyone)
    copies = []
    for k in far:
        to = lax.rem(me + k, count)
        copy = remote(normed.at[to], spread.at[core, chip], send_x.at[k], recv_x.at[k], to)
        copy.start()
        copies.append(copy)
    spread[core, chip] = normed[me]
    w_copy.wait()
    for k in far:
        sender = lax.rem(me + count - k, count)
        block = spread.at[lax.rem(sender, 2), sender // 2]
        remote(block, block, send_x.at[k], recv_x.at[k], sender).wait_recv()

    def multiply(which):
        def store(low, high, tile):
            terms[which, :, :, low:high] = tile.reshape(chips, rows, high - low)

        product(spread[which].reshape(chips * rows, part), w_ref, w_ref.shape[1], 1, store)

    multiply(other)
    order = far_first(pairs)
    firsts = {}
    for k in order + [0]:
        for w in range(2):
            j = lax.rem(pair + k, pairs) * 2 + (side if w else 1 - side)
            sems = send_a.at[2 * k + w], recv_a.at[2 * k + w]
            firsts[k, w] = remote(terms.at[other, j], sib.at[j], *sems, sibling)
            firsts[k, w].start()
    multiply(core)
    for k in order + [0]:
        to = lax.rem(pair + k, pairs)
        j = to * 2 + 1 - side
        firsts[k, 0].wait_recv()
        packed[0, to] = (terms[core, j] + sib[j]).astype(jnp.bfloat16)
        copy = remote(packed.at[0, to], arrived.at[0, to], send_b.at[k], recv_b.at[k], partner)
        copy.start()
        copies.append(copy)
    for k in order + [0]:
        to = lax.rem(pair + k, pairs)
        j = to * 2 + side
        firsts[k, 1].wait_recv()
        block = arrived.at[0, to]
        remote(block, block, send_b.at[k], recv_b.at[k], partner).wait_recv()
        total = terms[core, j] + sib[j] + arrived[0, to].astype(jnp.float32)
        if k:
            packed[1, to] = total.astype(jnp.bfloat16)
            sems = send_b.at[pairs + k], recv_b.at[pairs + k]
            copy = remote(packed.at[1, to], arrived.at[1, pair], *sems, j * 2 + core)
            copy.start()
            copies.append(copy)
    for k in order[::-1]:
        sender = lax.rem(pair + pairs - k, pairs)
        block = arrived.at[1, sender]
        sems = send_b.at[pairs + k], recv_b.at[pairs + k]
        remote(block, block, *sems, (sender * 2 + side) * 2 + core).wait_recv()
        total = total + arrived[1, sender].astype(jnp.float32)
    o_ref[...] = total.astype(jnp.bfloat16)
    for copy in list(firsts.values()) + copies:
        copy.wait_send()


def call(kernel, out, specs, scratch, collective_id, *args):
    return pl.pallas_call(
        kernel,
        out_shape=out,
        in_specs=[pl.BlockSpec(memory_space=space) for space in specs],
        out_specs=pl.BlockSpec(memory_space=VMEM),
        scratch_shapes=scratch,
        compiler_params=pltpu.CompilerParams(
            collective_id=collective_id, has_side_effects=True, vmem_limit_bytes=60 * 2**20
        ),
    )(*args)


def project(hidden, ln_gain, ln_bias, w_qkv, count, collective_id):
    rows = hidden.shape[0]
    part, width = w_qkv.shape
    chips = count // 2
    half = jnp.bfloat16
    return call(
        functools.partial(project_kernel, count),
        jax.ShapeDtypeStruct((rows, width), half),
        [VMEM, VMEM, VMEM, pl.ANY],
        [
            VMEM((part, width), half),
            VMEM((count, rows, part), half),
            VMEM((2, chips, rows, part), half),
            VMEM((2, chips, rows, width), jnp.float32),
            VMEM((chips, rows, width), jnp.float32),
            VMEM((2, chips // 2, rows, width), half),
            VMEM((2, chips // 2, rows, width), half),
            DMA,
        ]
        + [DMA((count,))] * 2
        + [DMA((chips,))] * 4,
        collective_id,
        hidden,
        ln_gain,
        ln_bias,
        w_qkv,
    )


def output_kernel(
    count,
    m_ref,
    h_ref,
    w_hbm,
    o_ref,
    w_ref,
    heads,
    columns,
    landed,
    w_sem,
    send_a,
    recv_a,
    send_y,
    recv_y,
    send_s,
    recv_s,
    send_x,
    recv_x,
):
    me = lax.axis_index("loop")
    core = lax.rem(me, 2)
    chip = me // 2
    other = 1 - core
    chips = count // 2
    pairs = chips // 2
    pair = chip // 2
    side = lax.rem(chip, 2)
    sibling = chip * 2 + other
    partner = (pair * 2 + 1 - side) * 2 + core
    rows, depth = m_ref.shape
    everyone = [lax.rem(me + k, count) for k in far_first(count)]
    hail(everyone)
    w_copy = pltpu.make_async_copy(w_hbm, w_ref, w_sem)
    w_copy.start()
    meet(everyone)
    order = far_first(pairs)[::-1]
    mine = heads.at[core, chip]
    copies = []

    def push(copy):
        copy.start()
        copies.append(copy)

    push(remote(m_ref, mine, send_y.at[0], recv_y.at[0], partner))
    for k in order[::-1]:
        to = (lax.rem(pair + k, pairs) * 2 + side) * 2 + core
        push(remote(m_ref, mine, send_a.at[k], recv_a.at[k], to))
    push(remote(m_ref, mine, send_s.at[0], recv_s.at[0], sibling))
    heads[core, chip] = m_ref[...]
    source = pair * 2 + 1 - side
    block = heads.at[core, source]
    remote(block, block, send_y.at[0], recv_y.at[0], partner).wait_recv()
    push(remote(block, block, send_s.at[pairs], recv_s.at[pairs], sibling))
    for k in order:
        source = lax.rem(pair + pairs - k, pairs) * 2 + side
        block = heads.at[core, source]
        remote(block, block, send_a.at[k], recv_a.at[k], partner).wait_recv()
        push(remote(block, block, send_y.at[k], recv_y.at[k], partner))
        push(remote(block, block, send_s.at[k], recv_s.at[k], sibling))
    for k in order:
        source = lax.rem(pair + pairs - k, pairs) * 2 + 1 - side
        block = heads.at[core, source]
        remote(block, block, send_y.at[k], recv_y.at[k], partner).wait_recv()
        push(remote(block, block, send_s.at[pairs + k], recv_s.at[pairs + k], sibling))
    w_copy.wait()

    def multiply(which):
        def store(low, high, tile):
            columns[which, :, :, low:high] = tile.astype(jnp.bfloat16).reshape(
                chips, rows, high - low
            )

        product(heads[which].reshape(chips * rows, depth), w_ref, w_ref.shape[0], 0, store)

    spans = far_first(chips)
    multiply(core)
    for k in spans:
        j = lax.rem(chip + k, chips)
        sems = send_x.at[k], recv_x.at[k]
        push(remote(columns.at[core, j], landed.at[me], *sems, j * 2 + core))
    landed[me] = columns[core, chip]
    for far in range(2):
        for k in [0] + order:
            source = lax.rem(pair + pairs - k, pairs) * 2 + (1 - side if far else side)
            block = heads.at[other, source]
            sem = far * pairs + k
            remote(block, block, send_s.at[sem], recv_s.at[sem], sibling).wait_recv()
    multiply(other)
    for k in spans + [0]:
        j = lax.rem(chip + k, chips)
        sems = send_x.at[chips + k], recv_x.at[chips + k]
        push(remote(columns.at[other, j], landed.at[me], *sems, j * 2 + other))
    for k in spans:
        sender = lax.rem(chip + chips - k, chips) * 2 + core
        block = landed.at[sender]
        remote(block, block, send_x.at[k], recv_x.at[k], sender).wait_recv()
    for k in spans + [0]:
        sender = lax.rem(chip + chips - k, chips) * 2 + other
        block = landed.at[sender]
        remote(block, block, send_x.at[chips + k], recv_x.at[chips + k], sender).wait_recv()
    part = landed.shape[2]
    for d in range(count):
        at = slice(d * part, (d + 1) * part)
        moved = h_ref[:, at].astype(jnp.float32) + landed[d].astype(jnp.float32)
        o_ref[:, at] = moved.astype(jnp.bfloat16)
    for copy in copies:
        copy.wait_send()


def output(mixed, hidden, w_out, count, collective_id):
    rows, depth = mixed.shape
    part = w_out.shape[1]
    turned = w_out.T
    chips = count // 2
    half = jnp.bfloat16
    return call(
        functools.partial(output_kernel, count),
        jax.ShapeDtypeStruct(hidden.shape, half),
        [VMEM, VMEM, pl.ANY],
        [
            VMEM((part, depth), half),
            VMEM((2, chips, rows, depth), half),
            VMEM((2, chips, rows, part), half),
            VMEM((count, rows, part), half),
            DMA,
        ]
        + [DMA((chips // 2,))] * 4
        + [DMA((chips,))] * 2
        + [DMA((count,))] * 2,
        collective_id,
        mixed,
        hidden,
        turned,
    )


def attend(queries, fresh_keys, fresh_values, cache_keys, cache_values, lengths):
    rows, steps, heads, head_dim = queries.shape
    context = cache_keys.shape[1]
    flat = queries.reshape(rows, steps * heads, head_dim)
    seen = jnp.arange(context, dtype=jnp.int32)[None, :] < lengths[:, None]
    old = jnp.einsum("rqe,rpe->rqp", flat, cache_keys, preferred_element_type=jnp.float32) * 0.125
    old = jnp.where(seen[:, None, :], old, -1e30)
    new = jnp.einsum("rqe,rte->rqt", flat, fresh_keys, preferred_element_type=jnp.float32) * 0.125
    step_of = jnp.arange(steps * heads, dtype=jnp.int32)[:, None] // heads
    seen_new = jnp.arange(steps, dtype=jnp.int32)[None, :] <= step_of
    new = jnp.where(seen_new[None], new, -1e30)
    maxima = jnp.maximum(
        jnp.max(old, axis=-1, keepdims=True), jnp.max(new, axis=-1, keepdims=True)
    )
    exp_old = jnp.exp(old - maxima)
    exp_new = jnp.exp(new - maxima)
    totals = jnp.sum(exp_old, axis=-1, keepdims=True) + jnp.sum(exp_new, axis=-1, keepdims=True)
    prob_old = (exp_old / totals).astype(jnp.bfloat16)
    prob_new = (exp_new / totals).astype(jnp.bfloat16)
    mixed = jnp.einsum("rqp,rpe->rqe", prob_old, cache_values, preferred_element_type=jnp.float32)
    mixed += jnp.einsum("rqt,rte->rqe", prob_new, fresh_values, preferred_element_type=jnp.float32)
    return mixed.reshape(rows, steps, heads * head_dim).astype(jnp.bfloat16)


def local(hidden, lengths, cache_keys, cache_values, ln_gain, ln_bias, w_qkv, w_out):
    steps, rows, width = hidden.shape
    head_dim = cache_keys.shape[2]
    heads = w_qkv.shape[1] // head_dim - 2
    count = lax.axis_size("loop")
    both = steps * rows
    projected = project(
        hidden.reshape(both, width), ln_gain, ln_bias, w_qkv, count, 0
    )
    projected = projected.reshape(steps, rows, -1).transpose(1, 0, 2)
    queries = projected[:, :, : heads * head_dim].reshape(rows, steps, heads, head_dim)
    fresh_keys = projected[:, :, heads * head_dim : (heads + 1) * head_dim]
    fresh_values = projected[:, :, (heads + 1) * head_dim :]
    mixed = attend(queries, fresh_keys, fresh_values, cache_keys, cache_values, lengths)
    mixed = mixed.transpose(1, 0, 2).reshape(steps * rows, -1)
    moved = output(mixed, hidden.reshape(both, width), w_out, count, 1)
    return moved.reshape(steps, rows, width)


def solution(mesh):
    return jax.shard_map(
        local,
        mesh=mesh,
        in_specs=(
            P(None, ("grp", "loop"), None),
            P(("grp", "loop")),
            P(("grp", "loop"), None, None),
            P(("grp", "loop"), None, None),
            P(),
            P(),
            P("loop", None),
            P(None, "loop"),
        ),
        out_specs=P(None, ("grp", "loop"), None),
        check_vma=False,
    )
```
